128 devices in a mesh: tp: 2 (over core), ep: 64 (over y, x, z).
Axes of the slice: x: 4, y: 4, z: 4, core: 2. Of those that a mesh axis runs over, the one named last changes fastest.
Arguments:
- tokens: bfloat16 [16384, 4096], P(('tp', 'ep')), may hold values from -6 to 6
- upstream: bfloat16 [16384, 4096], P(('tp', 'ep')), may hold values from -4 to 4
- routes: int32 [16384, 2], P(('tp', 'ep')), may hold values from 0 to 63, all different within a row; in each aligned block of 128 rows (0 to 127, 128 to 255, ...) at most 8 rows name the same one
- route_weights: float32 [16384, 2], P(('tp', 'ep')), may hold values from 0.1 to 1
- gate_weight: bfloat16 [64, 4096, 768], P('ep', None, 'tp'), may hold values from -0.09375 to 0.09375
- up_weight: bfloat16 [64, 4096, 768], P('ep', None, 'tp'), may hold values from -0.09375 to 0.09375
- down_weight: bfloat16 [64, 768, 4096], P('ep', 'tp'), may hold values from -0.21875 to 0.21875
Outputs:
- mixed: bfloat16 [16384, 4096], P(('tp', 'ep'))
- grad_tokens: bfloat16 [16384, 4096], P(('tp', 'ep'))
- grad_route: float32 [16384, 2], P(('tp', 'ep'))
- grad_gate: bfloat16 [64, 4096, 768], P('ep', None, 'tp')
- grad_up: bfloat16 [64, 4096, 768], P('ep', None, 'tp')
- grad_down: bfloat16 [64, 768, 4096], P('ep', 'tp')
The draws below stay inside these ranges and needn't reach their ends.
Inputs may be any that keep to these rules, and one draw needn't show every extreme that they name: `routes`: each row names 2 different experts. Among the 128 rows of one device no expert is named more than 8 times, a bound that some block reaches.
All inputs are finite; a program needn't handle non-finite values.
Results may differ from the reference program's by a relative error of at most 0.0072.
Values may be sent and summed in bfloat16 or wider, within the bound.
No kernel may reach another device: no remote copies, remote signals or barrier semaphores. Data moves between devices by JAX's collectives and lax.ppermute only.
A program may use at most 192 MiB of HBM per device.

```python
import math
import jax
import jax.numpy as jnp
import numpy as np
from jax import lax

D = 4096
HID = 768
TOP = 2
TOK_DEV = 128
EXPERTS = 64
CAP = 8
TOKENS = 16384
N_TP = 2
N_EP = 64


def shard_levels(stream_key, extent, split, least, largest):
    def one(dim, shards_of):
        steps = jax.random.uniform(jax.random.fold_in(jax.random.fold_in(stream_key, 6), dim), (shards_of,), jnp.float32, least / len(split), largest / len(split))
        return jnp.repeat(jnp.exp(steps), extent[dim] // shards_of).reshape((-1,) + (1,) * (len(extent) - dim - 1))

    level = one(*split[0])
    for cut in split[1:]:
        level = level * one(*cut)
    return level


def shared_out(rng, own, number, rows, count, top, bound, lean):
    ranking = jax.random.permutation(rng, count)
    packed, usual = shares(count, rows * top, bound, lean, True), shares(count, rows * top, bound, lean, False)
    places = jnp.arange(count)

    def named(tallies, offset_by):
        used = int((tallies > 0).sum())
        fixed = max(1, used // 4)
        passed = fixed + (places - fixed + offset_by * (used - fixed)) % max(1, count - fixed)
        return jnp.zeros((count,), jnp.int32).at[ranking[jnp.where(places < fixed, places, passed)]].set(jnp.asarray(tallies, jnp.int32))

    tallies = jnp.where(number % 4 == 0, named(packed, number // 4), named(usual, number - number // 4 - 1))
    mixed = jax.random.permutation(jax.random.fold_in(own, 3), count)
    giver, sink = mixed[0:count // 2 * 2:2], mixed[1:count // 2 * 2:2]
    margin = jnp.minimum(tallies[giver] - 1, bound - tallies[sink]) // 2
    margin = jnp.where((giver == ranking[0]) | (sink == ranking[0]) | (tallies[sink] == 0), 0, jnp.maximum(margin, 0))
    passed = jax.random.randint(jax.random.fold_in(own, 4), (count // 2,), 0, 1 << 20) % (margin + 1)
    tallies = tallies.at[giver].add(-passed).at[sink].add(passed)
    labels = jnp.searchsorted(jnp.cumsum(tallies), jnp.arange(rows * top), side="right").astype(jnp.int32)
    listing = labels.reshape(top, rows).T
    listing = listing[jax.random.permutation(jax.random.fold_in(own, 1), rows)]
    offset_by = jax.random.randint(jax.random.fold_in(own, 2), (rows, 1), 0, top)
    return jnp.take_along_axis(listing, (jnp.arange(top)[None, :] + offset_by) % top, axis=1)


def shares(amount, total, limit, skew, full):
    portions = [(1 << 20) // math.isqrt(rank ** skew) + 1 for rank in range(1, amount + 1)]
    largest = limit if full else min(limit, max(-(-total // amount), total * portions[0] // sum(portions)))
    least = 1 if total - largest >= amount - 1 else 0
    holding, rest = [largest] + [least] * (amount - 1), total - largest - least * (amount - 1)
    while rest > 0:
        movable = [i for i in range(1, amount) if holding[i] < largest] or [i for i in range(1, amount) if holding[i] < limit]
        whole, remaining = sum([portions[i] for i in movable]), rest
        for i in movable:
            more = min(limit - holding[i], max(1, remaining * portions[i] // whole), rest)
            holding[i] = holding[i] + more
            rest = rest - more
    return np.array(holding)


def scatter_about(stream_key, shape, deviation, bound, shards=(), kind=jnp.bfloat16):
    array = jax.random.normal(stream_key, shape, jnp.float32) * deviation
    if len(shards) > 0:
        array = shard_levels(stream_key, shape, shards, -0.22, 0.18) * array
    return jnp.clip(array, min=-bound, max=bound).astype(kind)


def setup_inputs(seed: int = 0) -> dict:
    keys = jax.random.split(jax.random.key(seed), 8)
    tokens = scatter_about(keys[0], (TOKENS, D), 1.0, 6.0, ((0, 128),))
    upstream = scatter_about(keys[1], (TOKENS, D), 0.25, 4.0, ((0, 128),))
    routes_keys = jax.random.split(jax.random.fold_in(keys[2], 1), TOKENS // TOK_DEV)
    routes_turns = jax.random.permutation(jax.random.fold_in(keys[2], 3), TOKENS // TOK_DEV)
    routes = jax.vmap(lambda own, number: shared_out(jax.random.fold_in(keys[2], 2), own, number, TOK_DEV, EXPERTS, TOP, CAP, 2))(routes_keys, routes_turns).reshape((TOKENS, TOP))
    route_weights = jnp.clip(0.1 + 0.9 * jax.random.uniform(keys[3], (TOKENS, TOP), jnp.float32) ** shard_levels(keys[3], (TOKENS, TOP), ((0, 128),), -0.2, 0.2), 0.1, 1.0)
    gate_weight = scatter_about(keys[4], (EXPERTS, D, HID), D ** -0.5, 0.09375, ((0, 64), (2, 2)))
    up_weight = scatter_about(keys[5], (EXPERTS, D, HID), D ** -0.5, 0.09375, ((0, 64), (2, 2)))
    down_weight = scatter_about(keys[6], (EXPERTS, HID, D), HID ** -0.5, 0.21875, ((0, 64), (1, 2)))
    return dict(tokens=tokens, upstream=upstream, routes=routes, route_weights=route_weights, gate_weight=gate_weight, up_weight=up_weight, down_weight=down_weight)


def slots_of(routes_block):
    expert_ids = jnp.arange(EXPERTS, dtype=jnp.int32)
    expert_hits = jnp.sum((routes_block[..., None] == expert_ids).astype(jnp.float32), axis=2)
    prior_counts = jnp.cumsum(expert_hits, axis=1) - expert_hits
    return jnp.take_along_axis(prior_counts, routes_block, axis=2).astype(jnp.int32)


def expert_pass(inputs, grad_rows, gate_mat, up_mat, down_mat):
    half_width = HID // N_TP
    gate_pre = jnp.dot(inputs, gate_mat, preferred_element_type=jnp.float32)
    up_pre = jnp.dot(inputs, up_mat, preferred_element_type=jnp.float32)
    sigmoid_gate = jax.nn.sigmoid(gate_pre)
    active = gate_pre * sigmoid_gate
    hidden = (active * up_pre).astype(jnp.bfloat16)
    d_hidden = jnp.dot(grad_rows, down_mat.T, preferred_element_type=jnp.float32)
    d_gate = (d_hidden * up_pre * sigmoid_gate * (1.0 + gate_pre * (1.0 - sigmoid_gate))).astype(jnp.bfloat16)
    d_up = (d_hidden * active).astype(jnp.bfloat16)
    out_total = jnp.zeros((inputs.shape[0], D), jnp.float32)
    back_total = jnp.zeros((inputs.shape[0], D), jnp.float32)
    for group_index in range(N_TP):
        start_col = group_index * half_width
        stop_col = start_col + half_width
        piece = jnp.dot(hidden[:, start_col:stop_col], down_mat[start_col:stop_col], preferred_element_type=jnp.float32).astype(jnp.bfloat16)
        out_total = out_total + lax.optimization_barrier(piece).astype(jnp.float32)
        piece = (jnp.dot(d_gate[:, start_col:stop_col], gate_mat[:, start_col:stop_col].T, preferred_element_type=jnp.float32)
                 + jnp.dot(d_up[:, start_col:stop_col], up_mat[:, start_col:stop_col].T, preferred_element_type=jnp.float32)).astype(jnp.bfloat16)
        back_total = back_total + lax.optimization_barrier(piece).astype(jnp.float32)
    grad_g = jnp.dot(inputs.T, d_gate, preferred_element_type=jnp.float32).astype(jnp.bfloat16)
    grad_u = jnp.dot(inputs.T, d_up, preferred_element_type=jnp.float32).astype(jnp.bfloat16)
    grad_d = jnp.dot(hidden.T, grad_rows, preferred_element_type=jnp.float32).astype(jnp.bfloat16)
    return out_total.astype(jnp.bfloat16), back_total.astype(jnp.bfloat16), grad_g, grad_u, grad_d


def reference(tokens, upstream, routes, route_weights, gate_weight, up_weight, down_weight):
    blocks = N_TP * N_EP
    slot_index = slots_of(routes.reshape(blocks, TOK_DEV, TOP)).reshape(TOKENS, TOP)
    block_of = (jnp.arange(TOKENS, dtype=jnp.int32) // TOK_DEV)[:, None]
    flat_pos = ((routes * blocks + block_of) * CAP + slot_index).reshape(-1)
    table_size = EXPERTS * blocks * CAP
    token_ids = jnp.broadcast_to(jnp.arange(TOKENS, dtype=jnp.int32)[:, None], (TOKENS, TOP)).reshape(-1)
    token_table = jnp.full((table_size,), TOKENS, jnp.int32).at[flat_pos].set(token_ids)
    assign_table = jnp.full((table_size,), TOKENS * TOP, jnp.int32).at[flat_pos].set(jnp.arange(TOKENS * TOP, dtype=jnp.int32))
    padded_tokens = jnp.concatenate([tokens, jnp.zeros((1, D), jnp.bfloat16)], axis=0)
    scaled_grads = (upstream.astype(jnp.float32)[:, None, :] * route_weights[:, :, None]).astype(jnp.bfloat16).reshape(TOKENS * TOP, D)
    padded_grads = jnp.concatenate([scaled_grads, jnp.zeros((1, D), jnp.bfloat16)], axis=0)

    def per_expert(carry, slab):
        out_asg, back_asg = carry
        token_rows, assign_rows, gate_mat, up_mat, down_mat = slab
        inputs = padded_tokens[token_rows]
        grad_rows = padded_grads[assign_rows]
        out_full, back_full, grad_g, grad_u, grad_d = expert_pass(inputs, grad_rows, gate_mat, up_mat, down_mat)
        out_asg = out_asg.at[assign_rows].set(out_full)
        back_asg = back_asg.at[assign_rows].set(back_full)
        return (out_asg, back_asg), (grad_g, grad_u, grad_d)

    start_state = (jnp.zeros((TOKENS * TOP + 1, D), jnp.bfloat16), jnp.zeros((TOKENS * TOP + 1, D), jnp.bfloat16))
    slabs = (token_table.reshape(EXPERTS, -1), assign_table.reshape(EXPERTS, -1), gate_weight, up_weight, down_weight)
    (out_asg, back_asg), (grad_gate, grad_up, grad_down) = lax.scan(per_expert, start_state, slabs)
    expert_rows = out_asg[:-1].reshape(TOKENS, TOP, D).astype(jnp.float32)
    mixed = jnp.sum(route_weights[:, :, None] * expert_rows, axis=1).astype(jnp.bfloat16)
    grad_route = jnp.sum(upstream.astype(jnp.float32)[:, None, :] * expert_rows, axis=2)
    grad_tokens = jnp.sum(back_asg[:-1].reshape(TOKENS, TOP, D).astype(jnp.float32), axis=1).astype(jnp.bfloat16)
    return (mixed, grad_tokens, grad_route, grad_gate, grad_up, grad_down)
```

```python
import functools

import jax
import jax.numpy as jnp
from jax import lax
from jax.experimental import pallas as pl
from jax.experimental.pallas import tpu as pltpu
from jax.sharding import PartitionSpec as P

TOP = 2
TOK_DEV = 128
SWAP = [(0, 1), (1, 0)]
PARTS = 4


def slot_rows(routes_ref, ep_size, capacity):
    tokens = routes_ref.shape[1]
    experts = lax.broadcasted_iota(jnp.int32, (ep_size, tokens), 0)
    named = [experts == routes_ref[k : k + 1, :] for k in range(TOP)]
    hits = functools.reduce(jnp.logical_or, named)
    ahead = lax.broadcasted_iota(jnp.int32, (tokens, tokens), 0)
    behind = lax.broadcasted_iota(jnp.int32, (tokens, tokens), 1)
    earlier = (ahead < behind).astype(jnp.bfloat16)
    prior = jnp.dot(hits.astype(jnp.bfloat16), earlier, preferred_element_type=jnp.float32)
    rows = []
    for k in range(TOP):
        slot = jnp.sum(jnp.where(named[k], prior, 0.0), axis=0, keepdims=True)
        rows.append(routes_ref[k : k + 1, :] * capacity + slot.astype(jnp.int32))
    return rows


def slot_masks(routes_ref, ep_size, capacity):
    tokens = routes_ref.shape[1]
    slots = lax.broadcasted_iota(jnp.int32, (ep_size * capacity, tokens), 0)
    return [slots == row for row in slot_rows(routes_ref, ep_size, capacity)]


def dispatch_tokens_kernel(ep_size, capacity, routes_ref, x_ref, out_ref):
    masks = slot_masks(routes_ref, ep_size, capacity)
    pick = functools.reduce(jnp.logical_or, masks).astype(jnp.bfloat16)
    out_ref[...] = jnp.dot(pick, x_ref[...], preferred_element_type=jnp.float32).astype(
        jnp.bfloat16
    )


def dispatch_grads_kernel(ep_size, capacity, routes_ref, weights_ref, x_ref, out_ref):
    masks = slot_masks(routes_ref, ep_size, capacity)
    pick = functools.reduce(jnp.logical_or, masks).astype(jnp.bfloat16)
    scale = sum(
        jnp.sum(jnp.where(masks[k], weights_ref[k : k + 1, :], 0.0), axis=1, keepdims=True)
        for k in range(TOP)
    )
    rows = jnp.dot(pick, x_ref[...], preferred_element_type=jnp.float32)
    out_ref[...] = (rows * scale).astype(jnp.bfloat16)


def split_weight(value):
    high = value.astype(jnp.bfloat16)
    low = (value - high.astype(jnp.float32)).astype(jnp.bfloat16)
    return high, low


def collect_dot(picked, rows):
    return lax.dot_general(
        picked, rows, (((0,), (0,)), ((), ())), preferred_element_type=jnp.float32
    )


def combine_outputs_kernel(
    ep_size, capacity, routes_ref, weights_ref, upstream_ref, rows_ref, mixed_ref, route_ref, acc
):
    step = pl.program_id(0)
    masks = slot_masks(routes_ref, ep_size, capacity)
    weighted = sum(
        jnp.where(masks[k], weights_ref[k : k + 1, :], 0.0) for k in range(TOP)
    )
    high, low = split_weight(weighted)
    rows = rows_ref[...]
    mixed_ref[...] = (collect_dot(high, rows) + collect_dot(low, rows)).astype(jnp.bfloat16)

    @pl.when(step == 0)
    def _():
        acc[...] = jnp.zeros_like(acc)

    acc[...] += lax.dot_general(
        rows, upstream_ref[...], (((1,), (1,)), ((), ())), preferred_element_type=jnp.float32
    )

    @pl.when(step == pl.num_programs(0) - 1)
    def _():
        for k in range(TOP):
            route_ref[k : k + 1, :] = jnp.sum(
                jnp.where(masks[k], acc[...], 0.0), axis=0, keepdims=True
            )


def combine_grads_kernel(ep_size, capacity, routes_ref, rows_ref, out_ref):
    masks = slot_masks(routes_ref, ep_size, capacity)
    pick = functools.reduce(jnp.logical_or, masks).astype(jnp.bfloat16)
    out_ref[...] = collect_dot(pick, rows_ref[...]).astype(jnp.bfloat16)


def whole(shape):
    return pl.BlockSpec(shape, lambda i: (0, 0))


def columns(rows, width):
    return pl.BlockSpec((rows, width), lambda i: (0, i))


def to_experts(rows, ep_size):
    blocks = rows.reshape(ep_size, -1, rows.shape[1])
    return lax.all_to_all(blocks, "ep", split_axis=0, concat_axis=0, tiled=True).reshape(rows.shape)


def swap(rows):
    return lax.ppermute(rows, "tp", SWAP)


def rows_dot(a, b):
    return jnp.dot(a, b, preferred_element_type=jnp.float32)


def turned_dot(a, b):
    return lax.dot_general(a, b, (((1,), (1,)), ((), ())), preferred_element_type=jnp.float32)


def weight_dot(a, b):
    return lax.dot_general(a, b, (((0,), (0,)), ((), ())), preferred_element_type=jnp.float32)


def add_up(step, acc, cols, value):
    @pl.when(step == 0)
    def _():
        acc[:, cols] = value

    @pl.when(step > 0)
    def _():
        acc[:, cols] += value


def hidden_steps(step, steps, x_ref, gate_ref, up_ref, gate_out, up_out, hidden_out):
    x = x_ref[...]
    full = slice(None)
    add_up(step, gate_out, full, rows_dot(x, gate_ref[...]))
    add_up(step, up_out, full, rows_dot(x, up_ref[...]))

    @pl.when(step == steps - 1)
    def _():
        gate_pre = gate_out[...]
        hidden_out[...] = (gate_pre * jax.nn.sigmoid(gate_pre) * up_out[...]).astype(jnp.bfloat16)


def put_parts(parts, value):
    rows = parts[0].shape[0]
    for i, part in enumerate(parts):
        part[...] = value[i * rows : (i + 1) * rows].astype(part.dtype)


def put_sums(out, value, others):
    rows = others[0].shape[0]
    for i, other in enumerate(others):
        at = slice(i * rows, (i + 1) * rows)
        out[at, :] = (value[at] + other[...].astype(jnp.float32)).astype(out.dtype)


def forward_near_kernel(steps, x_ref, gate_ref, up_ref, gate_out, up_out, hidden_out):
    hidden_steps(
        pl.program_id(0), steps, x_ref, gate_ref, up_ref, gate_out, up_out, hidden_out
    )


def forward_far_kernel(
    steps, x_ref, gate_ref, up_ref, down_ref, gate_out, up_out, hidden_out, *rows_out
):
    step = pl.program_id(0)

    @pl.when(step < steps)
    def _():
        hidden_steps(step, steps, x_ref, gate_ref, up_ref, gate_out, up_out, hidden_out)

    @pl.when(step >= steps)
    def _():
        put_parts(rows_out, rows_dot(hidden_out[...], down_ref[...]))


def forward_sum_kernel(hidden_ref, down_ref, *refs):
    put_sums(refs[-1], rows_dot(hidden_ref[...], down_ref[...]), refs[:-1])


def d_hidden_steps(step, steps, g_ref, down_ref, gate_ref, up_ref, d_gate_out, d_up_out, acc):
    add_up(step, acc, slice(None), turned_dot(g_ref[...], down_ref[...]))

    @pl.when(step == steps - 1)
    def _():
        gate_pre = gate_ref[...]
        d_hidden = acc[...]
        sigmoid_gate = jax.nn.sigmoid(gate_pre)
        d_gate_out[...] = (
            d_hidden * up_ref[...] * sigmoid_gate * (1.0 + gate_pre * (1.0 - sigmoid_gate))
        ).astype(jnp.bfloat16)
        d_up_out[...] = (d_hidden * gate_pre * sigmoid_gate).astype(jnp.bfloat16)


def backward_near_kernel(
    steps, g_ref, down_ref, gate_ref, up_ref, d_gate_out, d_up_out, acc
):
    d_hidden_steps(
        pl.program_id(0), steps, g_ref, down_ref, gate_ref, up_ref, d_gate_out, d_up_out, acc
    )


def backward_far_kernel(
    steps,
    g_ref,
    down_ref,
    gate_ref,
    up_ref,
    gate_mat_ref,
    up_mat_ref,
    d_gate_out,
    d_up_out,
    *refs,
):
    step = pl.program_id(0)
    rows_out, acc = refs[:-1], refs[-1]

    @pl.when(step < steps)
    def _():
        d_hidden_steps(
            step, steps, g_ref, down_ref, gate_ref, up_ref, d_gate_out, d_up_out, acc
        )

    @pl.when(step >= steps)
    def _():
        put_parts(
            rows_out,
            turned_dot(d_gate_out[...], gate_mat_ref[...])
            + turned_dot(d_up_out[...], up_mat_ref[...]),
        )


def backward_sum_kernel(d_gate_ref, d_up_ref, gate_mat_ref, up_mat_ref, *refs):
    value = turned_dot(d_gate_ref[...], gate_mat_ref[...]) + turned_dot(
        d_up_ref[...], up_mat_ref[...]
    )
    put_sums(refs[-1], value, refs[:-1])


def expert_calls(slots, width, units, block, params):
    steps = width // block
    bf16, f32 = jnp.bfloat16, jnp.float32
    first = lambda i: jnp.minimum(i, steps - 1)
    second = lambda i: jnp.maximum(i - steps, 0)
    same = lambda i: i
    wide = lambda rows, at: pl.BlockSpec((rows, block), lambda i: (0, at(i)))
    tall = lambda at: pl.BlockSpec((block, units), lambda i: (at(i), 0))
    held = whole((slots, units))
    parts = [wide(slots // PARTS, second)] * PARTS
    pieces = [jax.ShapeDtypeStruct((slots // PARTS, width), bf16)] * PARTS
    others = [wide(slots // PARTS, same)] * PARTS
    array = lambda columns, dtype: jax.ShapeDtypeStruct((slots, columns), dtype)
    few = pl.CostEstimate(flops=1, bytes_accessed=1, transcendentals=0)
    call = functools.partial(pl.pallas_call, compiler_params=params, cost_estimate=few)
    total = [pltpu.VMEM((slots, units), f32)]
    forward_near = call(
        functools.partial(forward_near_kernel, steps),
        grid=(steps,),
        in_specs=[wide(slots, same), tall(same), tall(same)],
        out_specs=[held, held, held],
        out_shape=[array(units, f32), array(units, f32), array(units, bf16)],
        name="forward_near",
    )
    forward_far = call(
        functools.partial(forward_far_kernel, steps),
        grid=(2 * steps,),
        in_specs=[wide(slots, first), tall(first), tall(first), wide(units, second)],
        out_specs=[held, held, held, *parts],
        out_shape=[array(units, f32), array(units, f32), array(units, bf16), *pieces],
        name="forward_far",
    )
    forward_sum = call(
        forward_sum_kernel,
        grid=(steps,),
        in_specs=[held, wide(units, same), *others],
        out_specs=wide(slots, same),
        out_shape=array(width, bf16),
        name="forward_sum",
    )
    backward_near = call(
        functools.partial(backward_near_kernel, steps),
        grid=(steps,),
        in_specs=[wide(slots, same), wide(units, same), held, held],
        out_specs=[held, held],
        out_shape=[array(units, bf16), array(units, bf16)],
        scratch_shapes=total,
        name="backward_near",
    )
    backward_far = call(
        functools.partial(backward_far_kernel, steps),
        grid=(2 * steps,),
        in_specs=[
            wide(slots, first), wide(units, first), held, held, tall(second), tall(second)
        ],
        out_specs=[held, held, *parts],
        out_shape=[array(units, bf16), array(units, bf16), *pieces],
        scratch_shapes=total,
        name="backward_far",
    )
    backward_sum = call(
        backward_sum_kernel,
        grid=(steps,),
        in_specs=[held, held, tall(same), tall(same), *others],
        out_specs=wide(slots, same),
        out_shape=array(width, bf16),
        name="backward_sum",
    )
    return forward_near, forward_far, forward_sum, backward_near, backward_far, backward_sum


def on_device(tokens, upstream, routes, route_weights, gate_weight, up_weight, down_weight):
    ep_size = lax.axis_size("ep")
    token_count, width = tokens.shape
    capacity = 2 * token_count * TOP // ep_size
    slots = ep_size * capacity
    block = min(1024, width)
    grid = (width // block,)
    routes_t = routes.T
    weights_t = route_weights.T
    small = whole((TOP, token_count))
    params = pltpu.CompilerParams(vmem_limit_bytes=40 * 1024 * 1024)
    sizes = (ep_size, capacity)

    sent_tokens = pl.pallas_call(
        functools.partial(dispatch_tokens_kernel, *sizes),
        grid=grid,
        in_specs=[small, columns(token_count, block)],
        out_specs=columns(slots, block),
        out_shape=jax.ShapeDtypeStruct((slots, width), jnp.bfloat16),
        compiler_params=params,
        name="dispatch_tokens",
    )(routes_t, tokens)
    sent_grads = pl.pallas_call(
        functools.partial(dispatch_grads_kernel, *sizes),
        grid=grid,
        in_specs=[small, small, columns(token_count, block)],
        out_specs=columns(slots, block),
        out_shape=jax.ShapeDtypeStruct((slots, width), jnp.bfloat16),
        compiler_params=params,
        name="dispatch_grads",
    )(routes_t, weights_t, upstream)

    gate_mat, up_mat, down_mat = gate_weight[0], up_weight[0], down_weight[0]

    calls = expert_calls(slots, width, gate_mat.shape[1], block, params)
    forward_near, forward_far, forward_sum, backward_near, backward_far, backward_sum = calls

    inputs = to_experts(sent_tokens, ep_size)
    inputs, sent_grads = lax.optimization_barrier((inputs, sent_grads))
    grads = to_experts(sent_grads, ep_size)
    inputs_far = swap(inputs)
    gate_near, up_near, hidden_near = forward_near(inputs, gate_mat, up_mat)
    gate_far, up_far, hidden_far, *out_far = forward_far(inputs_far, gate_mat, up_mat, down_mat)
    out = forward_sum(hidden_near, down_mat, *map(swap, out_far))
    grads, out = lax.optimization_barrier((grads, out))
    out_home = to_experts(out, ep_size)

    grads_far = swap(grads)
    d_gate_near, d_up_near = backward_near(grads, down_mat, gate_near, up_near)
    d_gate_far, d_up_far, *back_far = backward_far(
        grads_far, down_mat, gate_far, up_far, gate_mat, up_mat
    )
    back = backward_sum(d_gate_near, d_up_near, gate_mat, up_mat, *map(swap, back_far))
    out_home, back, d_up_near, hidden_near = lax.optimization_barrier(
        (out_home, back, d_up_near, hidden_near)
    )
    back_home = to_experts(back, ep_size)

    inputs_all = jnp.concatenate([inputs, inputs_far], axis=0)
    grads_all = jnp.concatenate([grads, grads_far], axis=0)
    hidden_all = jnp.concatenate([hidden_near, hidden_far], axis=0)
    d_gate_all = jnp.concatenate([d_gate_near, d_gate_far], axis=0)
    d_up_all = jnp.concatenate([d_up_near, d_up_far], axis=0)
    grad_down = weight_dot(hidden_all, grads_all).astype(jnp.bfloat16)
    grad_gate = weight_dot(inputs_all, d_gate_all).astype(jnp.bfloat16)
    grad_up = weight_dot(inputs_all, d_up_all).astype(jnp.bfloat16)

    mixed, grad_route = pl.pallas_call(
        functools.partial(combine_outputs_kernel, *sizes),
        grid=grid,
        in_specs=[small, small, columns(token_count, block), columns(slots, block)],
        out_specs=[columns(token_count, block), small],
        out_shape=[
            jax.ShapeDtypeStruct((token_count, width), jnp.bfloat16),
            jax.ShapeDtypeStruct((TOP, token_count), jnp.float32),
        ],
        scratch_shapes=[pltpu.VMEM((slots, token_count), jnp.float32)],
        compiler_params=params,
        name="combine_outputs",
    )(routes_t, weights_t, upstream, out_home)
    grad_tokens = pl.pallas_call(
        functools.partial(combine_grads_kernel, *sizes),
        grid=grid,
        in_specs=[small, columns(slots, block)],
        out_specs=columns(token_count, block),
        out_shape=jax.ShapeDtypeStruct((token_count, width), jnp.bfloat16),
        compiler_params=params,
        name="combine_grads",
    )(routes_t, back_home)
    return (mixed, grad_tokens, grad_route.T, grad_gate[None], grad_up[None], grad_down[None])


def solution(mesh):
    rows = P(("tp", "ep"), None)
    split_columns = P("ep", None, "tp")
    split_rows = P("ep", "tp", None)
    return jax.shard_map(
        on_device,
        mesh=mesh,
        in_specs=(rows, rows, rows, rows, split_columns, split_columns, split_rows),
        out_specs=(rows, rows, rows, split_columns, split_columns, split_rows),
        check_vma=False,
    )
```

```python
import functools

import jax
import jax.numpy as jnp
from jax import lax
from jax.experimental import pallas as pl
from jax.experimental.pallas import tpu as pltpu
from jax.sharding import PartitionSpec as P

TOP = 2
TOK_DEV = 128
SWAP = [(0, 1), (1, 0)]
FEW = pl.CostEstimate(flops=1, bytes_accessed=1, transcendentals=0)


def slot_rows(routes_ref, ep_size, capacity):
    tokens = routes_ref.shape[1]
    experts = lax.broadcasted_iota(jnp.int32, (ep_size, tokens), 0)
    named = [experts == routes_ref[k : k + 1, :] for k in range(TOP)]
    hits = functools.reduce(jnp.logical_or, named)
    ahead = lax.broadcasted_iota(jnp.int32, (tokens, tokens), 0)
    behind = lax.broadcasted_iota(jnp.int32, (tokens, tokens), 1)
    earlier = (ahead < behind).astype(jnp.bfloat16)
    prior = jnp.dot(hits.astype(jnp.bfloat16), earlier, preferred_element_type=jnp.float32)
    rows = []
    for k in range(TOP):
        slot = jnp.sum(jnp.where(named[k], prior, 0.0), axis=0, keepdims=True)
        rows.append(routes_ref[k : k + 1, :] * capacity + slot.astype(jnp.int32))
    return rows


def slot_masks(routes_ref, ep_size, capacity):
    tokens = routes_ref.shape[1]
    slots = lax.broadcasted_iota(jnp.int32, (ep_size * capacity, tokens), 0)
    return [slots == row for row in slot_rows(routes_ref, ep_size, capacity)]


def dispatch_tokens_kernel(ep_size, capacity, routes_ref, x_ref, out_ref):
    masks = slot_masks(routes_ref, ep_size, capacity)
    pick = functools.reduce(jnp.logical_or, masks).astype(jnp.bfloat16)
    out_ref[...] = jnp.dot(pick, x_ref[...], preferred_element_type=jnp.float32).astype(
        jnp.bfloat16
    )


def dispatch_grads_kernel(ep_size, capacity, routes_ref, weights_ref, x_ref, out_ref):
    masks = slot_masks(routes_ref, ep_size, capacity)
    pick = functools.reduce(jnp.logical_or, masks).astype(jnp.bfloat16)
    scale = sum(
        jnp.sum(jnp.where(masks[k], weights_ref[k : k + 1, :], 0.0), axis=1, keepdims=True)
        for k in range(TOP)
    )
    rows = jnp.dot(pick, x_ref[...], preferred_element_type=jnp.float32)
    out_ref[...] = (rows * scale).astype(jnp.bfloat16)


def split_weight(value):
    high = value.astype(jnp.bfloat16)
    low = (value - high.astype(jnp.float32)).astype(jnp.bfloat16)
    return high, low


def collect_dot(picked, rows):
    return lax.dot_general(
        picked, rows, (((0,), (0,)), ((), ())), preferred_element_type=jnp.float32
    )


def combine_outputs_kernel(
    ep_size, capacity, routes_ref, weights_ref, upstream_ref, rows_ref, mixed_ref, route_ref, acc
):
    step = pl.program_id(0)
    masks = slot_masks(routes_ref, ep_size, capacity)
    weighted = sum(
        jnp.where(masks[k], weights_ref[k : k + 1, :], 0.0) for k in range(TOP)
    )
    high, low = split_weight(weighted)
    rows = rows_ref[...]
    mixed_ref[...] = (collect_dot(high, rows) + collect_dot(low, rows)).astype(jnp.bfloat16)

    @pl.when(step == 0)
    def _():
        acc[...] = jnp.zeros_like(acc)

    acc[...] += lax.dot_general(
        rows, upstream_ref[...], (((1,), (1,)), ((), ())), preferred_element_type=jnp.float32
    )

    @pl.when(step == pl.num_programs(0) - 1)
    def _():
        for k in range(TOP):
            route_ref[k : k + 1, :] = jnp.sum(
                jnp.where(masks[k], acc[...], 0.0), axis=0, keepdims=True
            )


def combine_grads_kernel(ep_size, capacity, routes_ref, rows_ref, out_ref):
    masks = slot_masks(routes_ref, ep_size, capacity)
    pick = functools.reduce(jnp.logical_or, masks).astype(jnp.bfloat16)
    out_ref[...] = collect_dot(pick, rows_ref[...]).astype(jnp.bfloat16)


def rows_dot(a, b):
    return jnp.dot(a, b, preferred_element_type=jnp.float32)


def turned_dot(a, b):
    return lax.dot_general(a, b, (((1,), (1,)), ((), ())), preferred_element_type=jnp.float32)


def weight_dot(a, b):
    return lax.dot_general(a, b, (((0,), (0,)), ((), ())), preferred_element_type=jnp.float32)


def add_up(first, acc, value):
    @pl.when(first)
    def _():
        acc[...] = value

    @pl.when(jnp.logical_not(first))
    def _():
        acc[...] += value


def beside(*refs):
    return jnp.concatenate([ref[...] for ref in refs], axis=1)


def stacked(*refs):
    return jnp.concatenate([ref[...] for ref in refs], axis=0)


def forward_kernel(
    steps,
    x_ref,
    gate_a,
    gate_b,
    up_a,
    up_b,
    down_a,
    down_b,
    rows_out,
    pre,
    hidden_a,
    hidden_b,
    hidden,
):
    step = pl.program_id(0)
    units = gate_a.shape[1]
    both = 2 * units

    @pl.when(step < steps)
    def _():
        add_up(step == 0, pre, rows_dot(x_ref[...], beside(gate_a, gate_b, up_a, up_b)))

    @pl.when(step == steps - 1)
    def _():
        gate_pre = pre[:, :both]
        made = (gate_pre * jax.nn.sigmoid(gate_pre) * pre[:, both:]).astype(jnp.bfloat16)
        hidden[...] = made
        hidden_a[...] = made[:, :units]
        hidden_b[...] = made[:, units:]

    @pl.when(step >= steps)
    def _():
        rows_out[...] = rows_dot(hidden[...], stacked(down_a, down_b)).astype(jnp.bfloat16)


def backward_kernel(
    steps,
    g_ref,
    pre,
    down_a,
    down_b,
    gate_a,
    gate_b,
    up_a,
    up_b,
    rows_out,
    d_gate_a,
    d_gate_b,
    d_up_a,
    d_up_b,
    d_hidden,
    d_both,
):
    step = pl.program_id(0)
    units = gate_a.shape[1]
    both = 2 * units

    @pl.when(step < steps)
    def _():
        add_up(step == 0, d_hidden, turned_dot(g_ref[...], stacked(down_a, down_b)))

    @pl.when(step == steps - 1)
    def _():
        gate_pre = pre[:, :both]
        sigmoid_gate = jax.nn.sigmoid(gate_pre)
        d_rows = d_hidden[...]
        d_gate = (
            d_rows * pre[:, both:] * sigmoid_gate * (1.0 + gate_pre * (1.0 - sigmoid_gate))
        ).astype(jnp.bfloat16)
        d_up = (d_rows * gate_pre * sigmoid_gate).astype(jnp.bfloat16)
        d_both[:, :both] = d_gate
        d_both[:, both:] = d_up
        d_gate_a[...] = d_gate[:, :units]
        d_gate_b[...] = d_gate[:, units:]
        d_up_a[...] = d_up[:, :units]
        d_up_b[...] = d_up[:, units:]

    @pl.when(step >= steps)
    def _():
        rows_out[...] = turned_dot(d_both[...], beside(gate_a, gate_b, up_a, up_b)).astype(
            jnp.bfloat16
        )


def expert_calls(slots, width, units, block, params):
    steps = width // block
    bf16, f32 = jnp.bfloat16, jnp.float32
    first = lambda i: jnp.minimum(i, steps - 1)
    second = lambda i: jnp.maximum(i - steps, 0)
    rows = lambda at: pl.BlockSpec((slots, block), lambda i: (0, at(i)))
    wide = lambda at: pl.BlockSpec((units, block), lambda i: (0, at(i)))
    tall = lambda at: pl.BlockSpec((block, units), lambda i: (at(i), 0))
    held = whole((slots, units))
    pre = whole((slots, 4 * units))
    array = lambda columns, dtype: jax.ShapeDtypeStruct((slots, columns), dtype)
    call = functools.partial(
        pl.pallas_call, grid=(2 * steps,), compiler_params=params, cost_estimate=FEW
    )
    forward = call(
        functools.partial(forward_kernel, steps),
        in_specs=[rows(first)] + [tall(first)] * 4 + [wide(second)] * 2,
        out_specs=[rows(second), pre, held, held],
        out_shape=[array(width, bf16), array(4 * units, f32)] + [array(units, bf16)] * 2,
        scratch_shapes=[pltpu.VMEM((slots, 2 * units), bf16)],
        name="forward",
    )
    backward = call(
        functools.partial(backward_kernel, steps),
        in_specs=[rows(first), pre] + [wide(first)] * 2 + [tall(second)] * 4,
        out_specs=[rows(second)] + [held] * 4,
        out_shape=[array(width, bf16)] + [array(units, bf16)] * 4,
        scratch_shapes=[
            pltpu.VMEM((slots, 2 * units), f32), pltpu.VMEM((slots, 4 * units), bf16)
        ],
        name="backward",
    )
    return forward, backward


def gate_up_kernel(x_near, x_far, d_gate_near, d_gate_far, d_up_near, d_up_far, gate_out, up_out):
    units = d_gate_near.shape[1]
    total = weight_dot(x_near[...], beside(d_gate_near, d_up_near)) + weight_dot(
        x_far[...], beside(d_gate_far, d_up_far)
    )
    gate_out[...] = total[:, :units].astype(jnp.bfloat16)
    up_out[...] = total[:, units:].astype(jnp.bfloat16)


def down_kernel(g_near, g_far, hidden_near, hidden_far, down_out):
    down_out[...] = (
        weight_dot(hidden_near[...], g_near[...]) + weight_dot(hidden_far[...], g_far[...])
    ).astype(jnp.bfloat16)


def cost(products, *arrays):
    moved = sum(a.size * a.dtype.itemsize for a in arrays)
    return pl.CostEstimate(flops=2 * products, bytes_accessed=moved, transcendentals=0)


def grads_of_gate_up(near, far, d_gate, d_up, block, params):
    slots, width = near.shape
    units = d_gate[0].shape[1]
    held = whole((slots, units))
    tall = pl.BlockSpec((block, units), lambda i: (i, 0))
    rows = pl.BlockSpec((slots, block), lambda i: (0, i))
    return pl.pallas_call(
        gate_up_kernel,
        grid=(width // block,),
        in_specs=[rows, rows] + [held] * 4,
        out_specs=[tall, tall],
        out_shape=[jax.ShapeDtypeStruct((width, units), jnp.bfloat16)] * 2,
        compiler_params=params,
        cost_estimate=cost(4 * slots * width * units, near, far),
        name="grad_gate_up",
    )(near, far, *d_gate, *d_up)


def grads_of_down(near, far, hidden, block, params):
    slots, width = near.shape
    units = hidden[0].shape[1]
    held = whole((slots, units))
    rows = pl.BlockSpec((slots, block), lambda i: (0, i))
    return pl.pallas_call(
        down_kernel,
        grid=(width // block,),
        in_specs=[rows, rows, held, held],
        out_specs=pl.BlockSpec((units, block), lambda i: (0, i)),
        out_shape=jax.ShapeDtypeStruct((units, width), jnp.bfloat16),
        compiler_params=params,
        cost_estimate=cost(2 * slots * width * units, near, far),
        name="grad_down",
    )(near, far, *hidden)


def whole(shape):
    return pl.BlockSpec(shape, lambda i: (0, 0))


def columns(rows, width):
    return pl.BlockSpec((rows, width), lambda i: (0, i))


def to_experts(rows, ep_size):
    blocks = rows.reshape(ep_size, -1, rows.shape[1])
    return lax.all_to_all(blocks, "ep", split_axis=0, concat_axis=0, tiled=True).reshape(rows.shape)


def swap(rows):
    return lax.ppermute(rows, "tp", SWAP)


def on_device(tokens, upstream, routes, route_weights, gate_weight, up_weight, down_weight):
    ep_size = lax.axis_size("ep")
    token_count, width = tokens.shape
    capacity = 2 * token_count * TOP // ep_size
    slots = ep_size * capacity
    block = min(1024, width // 2)
    grid = (width // block,)
    routes_t = routes.T
    weights_t = route_weights.T
    small = whole((TOP, token_count))
    params = pltpu.CompilerParams(vmem_limit_bytes=56 * 1024 * 1024)
    sizes = (ep_size, capacity)

    sent_tokens = pl.pallas_call(
        functools.partial(dispatch_tokens_kernel, *sizes),
        grid=grid,
        in_specs=[small, columns(token_count, block)],
        out_specs=columns(slots, block),
        out_shape=jax.ShapeDtypeStruct((slots, width), jnp.bfloat16),
        compiler_params=params,
        name="dispatch_tokens",
    )(routes_t, tokens)
    sent_grads = pl.pallas_call(
        functools.partial(dispatch_grads_kernel, *sizes),
        grid=grid,
        in_specs=[small, small, columns(token_count, block)],
        out_specs=columns(slots, block),
        out_shape=jax.ShapeDtypeStruct((slots, width), jnp.bfloat16),
        compiler_params=params,
        name="dispatch_grads",
    )(routes_t, weights_t, upstream)

    gate_mat, up_mat, down_mat = gate_weight[0], up_weight[0], down_weight[0]
    gate = (gate_mat, swap(gate_mat))
    up = (up_mat, swap(up_mat))
    down = (down_mat, swap(down_mat))
    forward, backward = expert_calls(slots, width, gate_mat.shape[1], block, params)

    inputs = to_experts(sent_tokens, ep_size)
    inputs, sent_grads = lax.optimization_barrier((inputs, sent_grads))
    grads = to_experts(sent_grads, ep_size)
    out, pre, hidden_a, hidden_b = forward(inputs, *gate, *up, *down)
    grads, out = lax.optimization_barrier((grads, out))
    out_home = to_experts(out, ep_size)
    back, d_gate_a, d_gate_b, d_up_a, d_up_b = backward(grads, pre, *down, *gate, *up)
    out_home, back, d_up_a, d_gate_a, hidden_a = lax.optimization_barrier(
        (out_home, back, d_up_a, d_gate_a, hidden_a)
    )
    back_home = to_experts(back, ep_size)

    grad_gate, grad_up = grads_of_gate_up(
        inputs, swap(inputs), (d_gate_a, swap(d_gate_b)), (d_up_a, swap(d_up_b)), block, params
    )
    grad_down = grads_of_down(grads, swap(grads), (hidden_a, swap(hidden_b)), block, params)
    mixed, grad_route = pl.pallas_call(
        functools.partial(combine_outputs_kernel, *sizes),
        grid=grid,
        in_specs=[small, small, columns(token_count, block), columns(slots, block)],
        out_specs=[columns(token_count, block), small],
        out_shape=[
            jax.ShapeDtypeStruct((token_count, width), jnp.bfloat16),
            jax.ShapeDtypeStruct((TOP, token_count), jnp.float32),
        ],
        scratch_shapes=[pltpu.VMEM((slots, token_count), jnp.float32)],
        compiler_params=params,
        cost_estimate=cost(3 * token_count * slots * width, upstream, out_home),
        name="combine_outputs",
    )(routes_t, weights_t, upstream, out_home)
    grad_tokens = pl.pallas_call(
        functools.partial(combine_grads_kernel, *sizes),
        grid=grid,
        in_specs=[small, columns(slots, block)],
        out_specs=columns(token_count, block),
        out_shape=jax.ShapeDtypeStruct((token_count, width), jnp.bfloat16),
        compiler_params=params,
        name="combine_grads",
    )(routes_t, back_home)
    return (mixed, grad_tokens, grad_route.T, grad_gate[None], grad_up[None], grad_down[None])


def solution(mesh):
    rows = P(("tp", "ep"), None)
    split_columns = P("ep", None, "tp")
    split_rows = P("ep", "tp", None)
    return jax.shard_map(
        on_device,
        mesh=mesh,
        in_specs=(rows, rows, rows, rows, split_columns, split_columns, split_rows),
        out_specs=(rows, rows, rows, split_columns, split_columns, split_rows),
        check_vma=False,
    )
```

```python
import functools

import jax
import jax.numpy as jnp
from jax import lax
from jax.experimental import pallas as pl
from jax.experimental.pallas import tpu as pltpu
from jax.sharding import PartitionSpec as P

TOP = 2
TOK_DEV = 128
SWAP = [(0, 1), (1, 0)]
FEW = pl.CostEstimate(flops=1, bytes_accessed=1, transcendentals=0)


def slot_rows(routes_ref, ep_size, capacity):
    tokens = routes_ref.shape[1]
    experts = lax.broadcasted_iota(jnp.int32, (ep_size, tokens), 0)
    named = [experts == routes_ref[k : k + 1, :] for k in range(TOP)]
    hits = functools.reduce(jnp.logical_or, named)
    ahead = lax.broadcasted_iota(jnp.int32, (tokens, tokens), 0)
    behind = lax.broadcasted_iota(jnp.int32, (tokens, tokens), 1)
    earlier = (ahead < behind).astype(jnp.bfloat16)
    prior = jnp.dot(hits.astype(jnp.bfloat16), earlier, preferred_element_type=jnp.float32)
    rows = []
    for k in range(TOP):
        slot = jnp.sum(jnp.where(named[k], prior, 0.0), axis=0, keepdims=True)
        rows.append(routes_ref[k : k + 1, :] * capacity + slot.astype(jnp.int32))
    return rows


def slot_masks(routes_ref, ep_size, capacity):
    tokens = routes_ref.shape[1]
    slots = lax.broadcasted_iota(jnp.int32, (ep_size * capacity, tokens), 0)
    return [slots == row for row in slot_rows(routes_ref, ep_size, capacity)]


def dispatch_tokens_kernel(ep_size, capacity, routes_ref, x_ref, out_ref):
    masks = slot_masks(routes_ref, ep_size, capacity)
    pick = functools.reduce(jnp.logical_or, masks).astype(jnp.bfloat16)
    out_ref[...] = jnp.dot(pick, x_ref[...], preferred_element_type=jnp.float32).astype(
        jnp.bfloat16
    )


def dispatch_grads_kernel(ep_size, capacity, routes_ref, weights_ref, x_ref, out_ref):
    masks = slot_masks(routes_ref, ep_size, capacity)
    pick = functools.reduce(jnp.logical_or, masks).astype(jnp.bfloat16)
    scale = sum(
        jnp.sum(jnp.where(masks[k], weights_ref[k : k + 1, :], 0.0), axis=1, keepdims=True)
        for k in range(TOP)
    )
    rows = jnp.dot(pick, x_ref[...], preferred_element_type=jnp.float32)
    out_ref[...] = (rows * scale).astype(jnp.bfloat16)


def split_weight(value):
    high = value.astype(jnp.bfloat16)
    low = (value - high.astype(jnp.float32)).astype(jnp.bfloat16)
    return high, low


def collect_dot(picked, rows):
    return lax.dot_general(
        picked, rows, (((0,), (0,)), ((), ())), preferred_element_type=jnp.float32
    )


def combine_outputs_kernel(
    ep_size, capacity, routes_ref, weights_ref, upstream_ref, rows_ref, mixed_ref, route_ref, acc
):
    step = pl.program_id(0)
    masks = slot_masks(routes_ref, ep_size, capacity)
    weighted = sum(
        jnp.where(masks[k], weights_ref[k : k + 1, :], 0.0) for k in range(TOP)
    )
    high, low = split_weight(weighted)
    rows = rows_ref[...]
    mixed_ref[...] = (collect_dot(high, rows) + collect_dot(low, rows)).astype(jnp.bfloat16)

    @pl.when(step == 0)
    def _():
        acc[...] = jnp.zeros_like(acc)

    acc[...] += lax.dot_general(
        rows, upstream_ref[...], (((1,), (1,)), ((), ())), preferred_element_type=jnp.float32
    )

    @pl.when(step == pl.num_programs(0) - 1)
    def _():
        for k in range(TOP):
            route_ref[k : k + 1, :] = jnp.sum(
                jnp.where(masks[k], acc[...], 0.0), axis=0, keepdims=True
            )


def combine_grads_kernel(ep_size, capacity, routes_ref, rows_ref, out_ref):
    masks = slot_masks(routes_ref, ep_size, capacity)
    pick = functools.reduce(jnp.logical_or, masks).astype(jnp.bfloat16)
    out_ref[...] = collect_dot(pick, rows_ref[...]).astype(jnp.bfloat16)


def rows_dot(a, b):
    return jnp.dot(a, b, preferred_element_type=jnp.float32)


def turned_dot(a, b):
    return lax.dot_general(a, b, (((1,), (1,)), ((), ())), preferred_element_type=jnp.float32)


def weight_dot(a, b):
    return lax.dot_general(a, b, (((0,), (0,)), ((), ())), preferred_element_type=jnp.float32)


def add_up(first, acc, value):
    @pl.when(first)
    def _():
        acc[...] = value

    @pl.when(jnp.logical_not(first))
    def _():
        acc[...] += value


def beside(*refs):
    return jnp.concatenate([ref[...] for ref in refs], axis=1)


def stacked(*refs):
    return jnp.concatenate([ref[...] for ref in refs], axis=0)


def forward_kernel(
    steps,
    x_ref,
    gate_a,
    gate_b,
    up_a,
    up_b,
    down_a,
    down_b,
    rows_out,
    pre,
    hidden_a,
    hidden_b,
    hidden,
):
    step = pl.program_id(0)
    units = gate_a.shape[1]
    both = 2 * units

    @pl.when(step < steps)
    def _():
        add_up(step == 0, pre, rows_dot(x_ref[...], beside(gate_a, gate_b, up_a, up_b)))

    @pl.when(step == steps - 1)
    def _():
        gate_pre = pre[:, :both]
        made = (gate_pre * jax.nn.sigmoid(gate_pre) * pre[:, both:]).astype(jnp.bfloat16)
        hidden[...] = made
        hidden_a[...] = made[:, :units]
        hidden_b[...] = made[:, units:]

    @pl.when(step >= steps)
    def _():
        rows_out[...] = rows_dot(hidden[...], stacked(down_a, down_b)).astype(jnp.bfloat16)


def backward_kernel(
    steps,
    g_ref,
    pre,
    down_a,
    down_b,
    gate_a,
    gate_b,
    up_a,
    up_b,
    rows_out,
    d_gate_a,
    d_gate_b,
    d_up_a,
    d_up_b,
    d_hidden,
    d_both,
):
    step = pl.program_id(0)
    units = gate_a.shape[1]
    both = 2 * units

    @pl.when(step < steps)
    def _():
        add_up(step == 0, d_hidden, turned_dot(g_ref[...], stacked(down_a, down_b)))

    @pl.when(step == steps - 1)
    def _():
        gate_pre = pre[:, :both]
        sigmoid_gate = jax.nn.sigmoid(gate_pre)
        d_rows = d_hidden[...]
        d_gate = (
            d_rows * pre[:, both:] * sigmoid_gate * (1.0 + gate_pre * (1.0 - sigmoid_gate))
        ).astype(jnp.bfloat16)
        d_up = (d_rows * gate_pre * sigmoid_gate).astype(jnp.bfloat16)
        d_both[:, :both] = d_gate
        d_both[:, both:] = d_up
        d_gate_a[...] = d_gate[:, :units]
        d_gate_b[...] = d_gate[:, units:]
        d_up_a[...] = d_up[:, :units]
        d_up_b[...] = d_up[:, units:]

    @pl.when(step >= steps)
    def _():
        rows_out[...] = turned_dot(d_both[...], beside(gate_a, gate_b, up_a, up_b)).astype(
            jnp.bfloat16
        )


def expert_calls(slots, width, units, block, params):
    steps = width // block
    bf16, f32 = jnp.bfloat16, jnp.float32
    first = lambda i: jnp.minimum(i, steps - 1)
    second = lambda i: jnp.maximum(i - steps, 0)
    rows = lambda at: pl.BlockSpec((slots, block), lambda i: (0, at(i)))
    wide = lambda at: pl.BlockSpec((units, block), lambda i: (0, at(i)))
    tall = lambda at: pl.BlockSpec((block, units), lambda i: (at(i), 0))
    held = whole((slots, units))
    pre = whole((slots, 4 * units))
    array = lambda columns, dtype: jax.ShapeDtypeStruct((slots, columns), dtype)
    call = functools.partial(
        pl.pallas_call, grid=(2 * steps,), compiler_params=params, cost_estimate=FEW
    )
    forward = call(
        functools.partial(forward_kernel, steps),
        in_specs=[rows(first)] + [tall(first)] * 4 + [wide(second)] * 2,
        out_specs=[rows(second), pre, held, held],
        out_shape=[array(width, bf16), array(4 * units, f32)] + [array(units, bf16)] * 2,
        scratch_shapes=[pltpu.VMEM((slots, 2 * units), bf16)],
        name="forward",
    )
    backward = call(
        functools.partial(backward_kernel, steps),
        in_specs=[rows(first), pre] + [wide(first)] * 2 + [tall(second)] * 4,
        out_specs=[rows(second)] + [held] * 4,
        out_shape=[array(width, bf16)] + [array(units, bf16)] * 4,
        scratch_shapes=[
            pltpu.VMEM((slots, 2 * units), f32), pltpu.VMEM((slots, 4 * units), bf16)
        ],
        name="backward",
    )
    return forward, backward


def gate_up_kernel(x_near, x_far, d_gate_near, d_gate_far, d_up_near, d_up_far, gate_out, up_out):
    units = d_gate_near.shape[1]
    total = weight_dot(x_near[...], beside(d_gate_near, d_up_near)) + weight_dot(
        x_far[...], beside(d_gate_far, d_up_far)
    )
    gate_out[...] = total[:, :units].astype(jnp.bfloat16)
    up_out[...] = total[:, units:].astype(jnp.bfloat16)


def down_kernel(g_near, g_far, hidden_near, hidden_far, down_out):
    down_out[...] = (
        weight_dot(hidden_near[...], g_near[...]) + weight_dot(hidden_far[...], g_far[...])
    ).astype(jnp.bfloat16)


def cost(products, *arrays):
    moved = sum(a.size * a.dtype.itemsize for a in arrays)
    return pl.CostEstimate(flops=2 * products, bytes_accessed=moved, transcendentals=0)


def grads_of_gate_up(near, far, d_gate, d_up, block, params):
    slots, width = near.shape
    units = d_gate[0].shape[1]
    held = whole((slots, units))
    tall = pl.BlockSpec((block, units), lambda i: (i, 0))
    rows = pl.BlockSpec((slots, block), lambda i: (0, i))
    return pl.pallas_call(
        gate_up_kernel,
        grid=(width // block,),
        in_specs=[rows, rows] + [held] * 4,
        out_specs=[tall, tall],
        out_shape=[jax.ShapeDtypeStruct((width, units), jnp.bfloat16)] * 2,
        compiler_params=params,
        cost_estimate=cost(4 * slots * width * units, near, far),
        name="grad_gate_up",
    )(near, far, *d_gate, *d_up)


def grads_of_down(near, far, hidden, block, params):
    slots, width = near.shape
    units = hidden[0].shape[1]
    held = whole((slots, units))
    rows = pl.BlockSpec((slots, block), lambda i: (0, i))
    return pl.pallas_call(
        down_kernel,
        grid=(width // block,),
        in_specs=[rows, rows, held, held],
        out_specs=pl.BlockSpec((units, block), lambda i: (0, i)),
        out_shape=jax.ShapeDtypeStruct((units, width), jnp.bfloat16),
        compiler_params=params,
        cost_estimate=cost(2 * slots * width * units, near, far),
        name="grad_down",
    )(near, far, *hidden)


def whole(shape):
    return pl.BlockSpec(shape, lambda i: (0, 0))


def columns(rows, width):
    return pl.BlockSpec((rows, width), lambda i: (0, i))


def to_experts(rows, ep_size):
    blocks = rows.reshape(ep_size, -1, rows.shape[1])
    return lax.all_to_all(blocks, "ep", split_axis=0, concat_axis=0, tiled=True).reshape(rows.shape)


def swap(rows):
    return lax.ppermute(rows, "tp", SWAP)


def on_device(tokens, upstream, routes, route_weights, gate_weight, up_weight, down_weight):
    ep_size = lax.axis_size("ep")
    token_count, width = tokens.shape
    capacity = 2 * token_count * TOP // ep_size
    slots = ep_size * capacity
    block = min(1024, width // 2)
    broad = min(2048, width // 2)
    grid = (width // broad,)
    routes_t = routes.T
    weights_t = route_weights.T
    small = whole((TOP, token_count))
    params = pltpu.CompilerParams(vmem_limit_bytes=56 * 1024 * 1024)
    sizes = (ep_size, capacity)

    sent_tokens = pl.pallas_call(
        functools.partial(dispatch_tokens_kernel, *sizes),
        grid=grid,
        in_specs=[small, columns(token_count, broad)],
        out_specs=columns(slots, broad),
        out_shape=jax.ShapeDtypeStruct((slots, width), jnp.bfloat16),
        compiler_params=params,
        name="dispatch_tokens",
    )(routes_t, tokens)
    gate_mat, up_mat, down_mat = gate_weight[0], up_weight[0], down_weight[0]
    gate = (gate_mat, swap(gate_mat))
    up = (up_mat, swap(up_mat))
    down = (down_mat, swap(down_mat))
    gate_b, up_b, down_b, weights_late = lax.optimization_barrier(
        (gate[1], up[1], down[1], weights_t)
    )
    gate, up, down = (gate_mat, gate_b), (up_mat, up_b), (down_mat, down_b)
    sent_grads = pl.pallas_call(
        functools.partial(dispatch_grads_kernel, *sizes),
        grid=grid,
        in_specs=[small, small, columns(token_count, broad)],
        out_specs=columns(slots, broad),
        out_shape=jax.ShapeDtypeStruct((slots, width), jnp.bfloat16),
        compiler_params=params,
        name="dispatch_grads",
    )(routes_t, weights_late, upstream)

    forward, backward = expert_calls(slots, width, gate_mat.shape[1], block, params)

    inputs = to_experts(sent_tokens, ep_size)
    inputs, sent_grads = lax.optimization_barrier((inputs, sent_grads))
    grads = to_experts(sent_grads, ep_size)
    out, pre, hidden_a, hidden_b = forward(inputs, *gate, *up, *down)
    grads, out = lax.optimization_barrier((grads, out))
    out_home = to_experts(out, ep_size)
    back, d_gate_a, d_gate_b, d_up_a, d_up_b = backward(grads, pre, *down, *gate, *up)
    out_home, back, d_up_a, d_gate_a, hidden_a = lax.optimization_barrier(
        (out_home, back, d_up_a, d_gate_a, hidden_a)
    )
    back_home = to_experts(back, ep_size)

    grad_gate, grad_up = grads_of_gate_up(
        inputs, swap(inputs), (d_gate_a, swap(d_gate_b)), (d_up_a, swap(d_up_b)), block, params
    )
    grad_down = grads_of_down(grads, swap(grads), (hidden_a, swap(hidden_b)), block, params)
    mixed, grad_route = pl.pallas_call(
        functools.partial(combine_outputs_kernel, *sizes),
        grid=grid,
        in_specs=[small, small, columns(token_count, broad), columns(slots, broad)],
        out_specs=[columns(token_count, broad), small],
        out_shape=[
            jax.ShapeDtypeStruct((token_count, width), jnp.bfloat16),
            jax.ShapeDtypeStruct((TOP, token_count), jnp.float32),
        ],
        scratch_shapes=[pltpu.VMEM((slots, token_count), jnp.float32)],
        compiler_params=params,
        cost_estimate=cost(3 * token_count * slots * width, upstream, out_home),
        name="combine_outputs",
    )(routes_t, weights_t, upstream, out_home)
    grad_tokens = pl.pallas_call(
        functools.partial(combine_grads_kernel, *sizes),
        grid=grid,
        in_specs=[small, columns(slots, broad)],
        out_specs=columns(token_count, broad),
        out_shape=jax.ShapeDtypeStruct((token_count, width), jnp.bfloat16),
        compiler_params=params,
        name="combine_grads",
    )(routes_t, back_home)
    return (mixed, grad_tokens, grad_route.T, grad_gate[None], grad_up[None], grad_down[None])


def solution(mesh):
    rows = P(("tp", "ep"), None)
    split_columns = P("ep", None, "tp")
    split_rows = P("ep", "tp", None)
    return jax.shard_map(
        on_device,
        mesh=mesh,
        in_specs=(rows, rows, rows, rows, split_columns, split_columns, split_rows),
        out_specs=(rows, rows, rows, split_columns, split_columns, split_rows),
        check_vma=False,
    )
```

```python
import functools

import jax
import jax.numpy as jnp
from jax import lax
from jax.experimental import pallas as pl
from jax.experimental.pallas import tpu as pltpu
from jax.sharding import PartitionSpec as P

TOP = 2
TOK_DEV = 128
SWAP = [(0, 1), (1, 0)]
FEW = pl.CostEstimate(flops=1, bytes_accessed=1, transcendentals=0)


def slot_rows(routes_ref, ep_size, capacity):
    tokens = routes_ref.shape[1]
    experts = lax.broadcasted_iota(jnp.int32, (ep_size, tokens), 0)
    named = [experts == routes_ref[k : k + 1, :] for k in range(TOP)]
    hits = functools.reduce(jnp.logical_or, named)
    ahead = lax.broadcasted_iota(jnp.int32, (tokens, tokens), 0)
    behind = lax.broadcasted_iota(jnp.int32, (tokens, tokens), 1)
    earlier = (ahead < behind).astype(jnp.bfloat16)
    prior = jnp.dot(hits.astype(jnp.bfloat16), earlier, preferred_element_type=jnp.float32)
    rows = []
    for k in range(TOP):
        slot = jnp.sum(jnp.where(named[k], prior, 0.0), axis=0, keepdims=True)
        rows.append(routes_ref[k : k + 1, :] * capacity + slot.astype(jnp.int32))
    return rows


def slot_masks(routes_ref, ep_size, capacity):
    tokens = routes_ref.shape[1]
    slots = lax.broadcasted_iota(jnp.int32, (ep_size * capacity, tokens), 0)
    return [slots == row for row in slot_rows(routes_ref, ep_size, capacity)]


def place_grads(sizes, routes_ref, weights_ref, g_ref, rows, rows_hbm, sems):
    masks = slot_masks(routes_ref, *sizes)
    pick = functools.reduce(jnp.logical_or, masks).astype(jnp.bfloat16)
    scale = sum(
        jnp.sum(jnp.where(masks[k], weights_ref[k : k + 1, :], 0.0), axis=1, keepdims=True)
        for k in range(TOP)
    )
    half = rows.shape[1] // 2
    copies = []
    for i in range(2):
        at = pl.ds(i * half, half)
        placed = jnp.dot(pick, g_ref[:, at], preferred_element_type=jnp.float32)
        rows[:, at] = (placed * scale).astype(jnp.bfloat16)
        copies.append(pltpu.make_async_copy(rows.at[:, at], rows_hbm.at[:, at], sems.at[1 + i]))
        copies[-1].start()
    for copy in copies:
        copy.wait()


def dispatch_tokens_kernel(
    sizes, routes_ref, weights_ref, x_ref, g_hbm, out_ref, early_hbm, pick_ref, g_ref, rows, sems
):
    step = pl.program_id(0)
    first = step == 0
    early = lax.axis_index("tp") == 0
    load = pltpu.make_async_copy(g_hbm, g_ref, sems.at[0])

    @pl.when(jnp.logical_and(early, first))
    def _():
        load.start()

    @pl.when(first)
    def _():
        masks = slot_masks(routes_ref, *sizes)
        pick_ref[...] = functools.reduce(jnp.logical_or, masks).astype(jnp.bfloat16)

    out_ref[...] = jnp.dot(
        pick_ref[...], x_ref[...], preferred_element_type=jnp.float32
    ).astype(jnp.bfloat16)

    @pl.when(jnp.logical_and(early, step == pl.num_programs(0) - 1))
    def _():
        load.wait()
        place_grads(sizes, routes_ref, weights_ref, g_ref, rows, early_hbm, sems)


def dispatch_grads_kernel(
    sizes, routes_ref, weights_ref, g_hbm, early_hbm, out_hbm, g_ref, rows, sems
):
    @pl.when(lax.axis_index("tp") != 0)
    def _():
        load = pltpu.make_async_copy(g_hbm, g_ref, sems.at[0])
        load.start()
        load.wait()
        place_grads(sizes, routes_ref, weights_ref, g_ref, rows, out_hbm, sems)


def split_weight(value):
    high = value.astype(jnp.bfloat16)
    low = (value - high.astype(jnp.float32)).astype(jnp.bfloat16)
    return high, low


def collect_dot(picked, rows):
    return lax.dot_general(
        picked, rows, (((0,), (0,)), ((), ())), preferred_element_type=jnp.float32
    )


def combine_outputs_kernel(
    ep_size, capacity, routes_ref, weights_ref, upstream_ref, rows_ref, mixed_ref, route_ref, acc
):
    step = pl.program_id(0)
    masks = slot_masks(routes_ref, ep_size, capacity)
    weighted = sum(
        jnp.where(masks[k], weights_ref[k : k + 1, :], 0.0) for k in range(TOP)
    )
    high, low = split_weight(weighted)
    rows = rows_ref[...]
    mixed_ref[...] = (collect_dot(high, rows) + collect_dot(low, rows)).astype(jnp.bfloat16)

    @pl.when(step == 0)
    def _():
        acc[...] = jnp.zeros_like(acc)

    acc[...] += lax.dot_general(
        rows, upstream_ref[...], (((1,), (1,)), ((), ())), preferred_element_type=jnp.float32
    )

    @pl.when(step == pl.num_programs(0) - 1)
    def _():
        for k in range(TOP):
            route_ref[k : k + 1, :] = jnp.sum(
                jnp.where(masks[k], acc[...], 0.0), axis=0, keepdims=True
            )


def combine_grads_kernel(ep_size, capacity, routes_ref, rows_ref, out_ref):
    masks = slot_masks(routes_ref, ep_size, capacity)
    pick = functools.reduce(jnp.logical_or, masks).astype(jnp.bfloat16)
    out_ref[...] = collect_dot(pick, rows_ref[...]).astype(jnp.bfloat16)


def rows_dot(a, b):
    return jnp.dot(a, b, preferred_element_type=jnp.float32)


def turned_dot(a, b):
    return lax.dot_general(a, b, (((1,), (1,)), ((), ())), preferred_element_type=jnp.float32)


def weight_dot(a, b):
    return lax.dot_general(a, b, (((0,), (0,)), ((), ())), preferred_element_type=jnp.float32)


def add_up(first, acc, value):
    @pl.when(first)
    def _():
        acc[...] = value

    @pl.when(jnp.logical_not(first))
    def _():
        acc[...] += value


def beside(*refs):
    return jnp.concatenate([ref[...] for ref in refs], axis=1)


def stacked(*refs):
    return jnp.concatenate([ref[...] for ref in refs], axis=0)


def forward_kernel(
    steps,
    x_ref,
    gate_a,
    gate_b,
    up_a,
    up_b,
    down_a,
    down_b,
    rows_out,
    pre,
    hidden_a,
    hidden_b,
    hidden,
):
    step = pl.program_id(0)
    units = gate_a.shape[1]
    both = 2 * units

    @pl.when(step < steps)
    def _():
        add_up(step == 0, pre, rows_dot(x_ref[...], beside(gate_a, gate_b, up_a, up_b)))

    @pl.when(step == steps - 1)
    def _():
        gate_pre = pre[:, :both]
        made = (gate_pre * jax.nn.sigmoid(gate_pre) * pre[:, both:]).astype(jnp.bfloat16)
        hidden[...] = made
        hidden_a[...] = made[:, :units]
        hidden_b[...] = made[:, units:]

    @pl.when(step >= steps)
    def _():
        rows_out[...] = rows_dot(hidden[...], stacked(down_a, down_b)).astype(jnp.bfloat16)


def backward_kernel(
    steps,
    g_ref,
    pre,
    down_a,
    down_b,
    gate_a,
    gate_b,
    up_a,
    up_b,
    rows_out,
    d_gate_a,
    d_gate_b,
    d_up_a,
    d_up_b,
    d_hidden,
    d_both,
):
    step = pl.program_id(0)
    units = gate_a.shape[1]
    both = 2 * units

    @pl.when(step < steps)
    def _():
        add_up(step == 0, d_hidden, turned_dot(g_ref[...], stacked(down_a, down_b)))

    @pl.when(step == steps - 1)
    def _():
        gate_pre = pre[:, :both]
        sigmoid_gate = jax.nn.sigmoid(gate_pre)
        d_rows = d_hidden[...]
        d_gate = (
            d_rows * pre[:, both:] * sigmoid_gate * (1.0 + gate_pre * (1.0 - sigmoid_gate))
        ).astype(jnp.bfloat16)
        d_up = (d_rows * gate_pre * sigmoid_gate).astype(jnp.bfloat16)
        d_both[:, :both] = d_gate
        d_both[:, both:] = d_up
        d_gate_a[...] = d_gate[:, :units]
        d_gate_b[...] = d_gate[:, units:]
        d_up_a[...] = d_up[:, :units]
        d_up_b[...] = d_up[:, units:]

    @pl.when(step >= steps)
    def _():
        rows_out[...] = turned_dot(d_both[...], beside(gate_a, gate_b, up_a, up_b)).astype(
            jnp.bfloat16
        )


def expert_calls(slots, width, units, block, params):
    steps = width // block
    bf16, f32 = jnp.bfloat16, jnp.float32
    first = lambda i: jnp.minimum(i, steps - 1)
    second = lambda i: jnp.maximum(i - steps, 0)
    rows = lambda at: pl.BlockSpec((slots, block), lambda i: (0, at(i)))
    wide = lambda at: pl.BlockSpec((units, block), lambda i: (0, at(i)))
    tall = lambda at: pl.BlockSpec((block, units), lambda i: (at(i), 0))
    held = whole((slots, units))
    pre = whole((slots, 4 * units))
    array = lambda columns, dtype: jax.ShapeDtypeStruct((slots, columns), dtype)
    call = functools.partial(
        pl.pallas_call, grid=(2 * steps,), compiler_params=params, cost_estimate=FEW
    )
    forward = call(
        functools.partial(forward_kernel, steps),
        in_specs=[rows(first)] + [tall(first)] * 4 + [wide(second)] * 2,
        out_specs=[rows(second), pre, held, held],
        out_shape=[array(width, bf16), array(4 * units, f32)] + [array(units, bf16)] * 2,
        scratch_shapes=[pltpu.VMEM((slots, 2 * units), bf16)],
        name="forward",
    )
    backward = call(
        functools.partial(backward_kernel, steps),
        in_specs=[rows(first), pre] + [wide(first)] * 2 + [tall(second)] * 4,
        out_specs=[rows(second)] + [held] * 4,
        out_shape=[array(width, bf16)] + [array(units, bf16)] * 4,
        scratch_shapes=[
            pltpu.VMEM((slots, 2 * units), f32), pltpu.VMEM((slots, 4 * units), bf16)
        ],
        name="backward",
    )
    return forward, backward


def gate_up_kernel(x_near, x_far, d_gate_near, d_gate_far, d_up_near, d_up_far, gate_out, up_out):
    units = d_gate_near.shape[1]
    total = weight_dot(x_near[...], beside(d_gate_near, d_up_near)) + weight_dot(
        x_far[...], beside(d_gate_far, d_up_far)
    )
    gate_out[...] = total[:, :units].astype(jnp.bfloat16)
    up_out[...] = total[:, units:].astype(jnp.bfloat16)


def down_kernel(g_near, g_far, hidden_near, hidden_far, down_out):
    down_out[...] = (
        weight_dot(hidden_near[...], g_near[...]) + weight_dot(hidden_far[...], g_far[...])
    ).astype(jnp.bfloat16)


def cost(products, *arrays):
    moved = sum(a.size * a.dtype.itemsize for a in arrays)
    return pl.CostEstimate(flops=2 * products, bytes_accessed=moved, transcendentals=0)


def grads_of_gate_up(near, far, d_gate, d_up, block, params):
    slots, width = near.shape
    units = d_gate[0].shape[1]
    held = whole((slots, units))
    tall = pl.BlockSpec((block, units), lambda i: (i, 0))
    rows = pl.BlockSpec((slots, block), lambda i: (0, i))
    return pl.pallas_call(
        gate_up_kernel,
        grid=(width // block,),
        in_specs=[rows, rows] + [held] * 4,
        out_specs=[tall, tall],
        out_shape=[jax.ShapeDtypeStruct((width, units), jnp.bfloat16)] * 2,
        compiler_params=params,
        cost_estimate=cost(4 * slots * width * units, near, far),
        name="grad_gate_up",
    )(near, far, *d_gate, *d_up)


def grads_of_down(near, far, hidden, block, params):
    slots, width = near.shape
    units = hidden[0].shape[1]
    held = whole((slots, units))
    rows = pl.BlockSpec((slots, block), lambda i: (0, i))
    return pl.pallas_call(
        down_kernel,
        grid=(width // block,),
        in_specs=[rows, rows, held, held],
        out_specs=pl.BlockSpec((units, block), lambda i: (0, i)),
        out_shape=jax.ShapeDtypeStruct((units, width), jnp.bfloat16),
        compiler_params=params,
        cost_estimate=cost(2 * slots * width * units, near, far),
        name="grad_down",
    )(near, far, *hidden)


def whole(shape):
    return pl.BlockSpec(shape, lambda i: (0, 0))


def columns(rows, width):
    return pl.BlockSpec((rows, width), lambda i: (0, i))


def to_experts(rows, ep_size):
    blocks = rows.reshape(ep_size, -1, rows.shape[1])
    return lax.all_to_all(blocks, "ep", split_axis=0, concat_axis=0, tiled=True).reshape(rows.shape)


def swap(rows):
    return lax.ppermute(rows, "tp", SWAP)


def on_device(tokens, upstream, routes, route_weights, gate_weight, up_weight, down_weight):
    ep_size = lax.axis_size("ep")
    token_count, width = tokens.shape
    capacity = 2 * token_count * TOP // ep_size
    slots = ep_size * capacity
    block = min(1024, width // 2)
    broad = min(2048, width // 2)
    grid = (width // broad,)
    routes_t = routes.T
    weights_t = route_weights.T
    small = whole((TOP, token_count))
    params = pltpu.CompilerParams(vmem_limit_bytes=56 * 1024 * 1024)
    sizes = (ep_size, capacity)

    anywhere = pl.BlockSpec(memory_space=pl.ANY)
    inside = pl.BlockSpec(memory_space=pltpu.VMEM)
    sent = jax.ShapeDtypeStruct((slots, width), jnp.bfloat16)
    place = [
        pltpu.VMEM((token_count, width), jnp.bfloat16),
        pltpu.VMEM((slots, width), jnp.bfloat16),
        pltpu.SemaphoreType.DMA((3,)),
    ]
    sent_tokens, early_grads = pl.pallas_call(
        functools.partial(dispatch_tokens_kernel, sizes),
        grid=grid,
        in_specs=[small, small, columns(token_count, broad), anywhere],
        out_specs=[columns(slots, broad), anywhere],
        out_shape=[sent, sent],
        scratch_shapes=[pltpu.VMEM((slots, token_count), jnp.bfloat16)] + place,
        compiler_params=params,
        name="dispatch_tokens",
    )(routes_t, weights_t, tokens, upstream)
    gate_mat, up_mat, down_mat = gate_weight[0], up_weight[0], down_weight[0]
    gate = (gate_mat, swap(gate_mat))
    up = (up_mat, swap(up_mat))
    down = (down_mat, swap(down_mat))
    gate_b, up_b, down_b, weights_late = lax.optimization_barrier(
        (gate[1], up[1], down[1], weights_t)
    )
    gate, up, down = (gate_mat, gate_b), (up_mat, up_b), (down_mat, down_b)
    sent_grads = pl.pallas_call(
        functools.partial(dispatch_grads_kernel, sizes),
        in_specs=[inside, inside, anywhere, anywhere],
        out_specs=anywhere,
        out_shape=sent,
        input_output_aliases={3: 0},
        scratch_shapes=place,
        compiler_params=params,
        name="dispatch_grads",
    )(routes_t, weights_late, upstream, early_grads)
    forward, backward = expert_calls(slots, width, gate_mat.shape[1], block, params)

    inputs = to_experts(sent_tokens, ep_size)
    inputs, sent_grads = lax.optimization_barrier((inputs, sent_grads))
    grads = to_experts(sent_grads, ep_size)
    out, pre, hidden_a, hidden_b = forward(inputs, *gate, *up, *down)
    grads, out = lax.optimization_barrier((grads, out))
    out_home = to_experts(out, ep_size)
    back, d_gate_a, d_gate_b, d_up_a, d_up_b = backward(grads, pre, *down, *gate, *up)
    out_home, back, d_up_a, d_gate_a, hidden_a = lax.optimization_barrier(
        (out_home, back, d_up_a, d_gate_a, hidden_a)
    )
    back_home = to_experts(back, ep_size)

    grad_gate, grad_up = grads_of_gate_up(
        inputs, swap(inputs), (d_gate_a, swap(d_gate_b)), (d_up_a, swap(d_up_b)), block, params
    )
    grad_down = grads_of_down(grads, swap(grads), (hidden_a, swap(hidden_b)), block, params)
    mixed, grad_route = pl.pallas_call(
        functools.partial(combine_outputs_kernel, *sizes),
        grid=grid,
        in_specs=[small, small, columns(token_count, broad), columns(slots, broad)],
        out_specs=[columns(token_count, broad), small],
        out_shape=[
            jax.ShapeDtypeStruct((token_count, width), jnp.bfloat16),
            jax.ShapeDtypeStruct((TOP, token_count), jnp.float32),
        ],
        scratch_shapes=[pltpu.VMEM((slots, token_count), jnp.float32)],
        compiler_params=params,
        cost_estimate=cost(3 * token_count * slots * width, upstream, out_home),
        name="combine_outputs",
    )(routes_t, weights_t, upstream, out_home)
    grad_tokens = pl.pallas_call(
        functools.partial(combine_grads_kernel, *sizes),
        grid=grid,
        in_specs=[small, columns(slots, broad)],
        out_specs=columns(token_count, broad),
        out_shape=jax.ShapeDtypeStruct((token_count, width), jnp.bfloat16),
        compiler_params=params,
        name="combine_grads",
    )(routes_t, back_home)
    return (mixed, grad_tokens, grad_route.T, grad_gate[None], grad_up[None], grad_down[None])


def solution(mesh):
    rows = P(("tp", "ep"), None)
    split_columns = P("ep", None, "tp")
    split_rows = P("ep", "tp", None)
    return jax.shard_map(
        on_device,
        mesh=mesh,
        in_specs=(rows, rows, rows, rows, split_columns, split_columns, split_rows),
        out_specs=(rows, rows, rows, split_columns, split_columns, split_rows),
        check_vma=False,
    )
```

```python
import functools

import jax
import jax.numpy as jnp
from jax import lax
from jax.experimental import pallas as pl
from jax.experimental.pallas import tpu as pltpu
from jax.sharding import PartitionSpec as P

TOP = 2
TOK_DEV = 128
SWAP = [(0, 1), (1, 0)]
FEW = pl.CostEstimate(flops=1, bytes_accessed=1, transcendentals=0)


def slot_rows(routes_ref, ep_size, capacity):
    tokens = routes_ref.shape[1]
    experts = lax.broadcasted_iota(jnp.int32, (ep_size, tokens), 0)
    named = [experts == routes_ref[k : k + 1, :] for k in range(TOP)]
    hits = functools.reduce(jnp.logical_or, named)
    ahead = lax.broadcasted_iota(jnp.int32, (tokens, tokens), 0)
    behind = lax.broadcasted_iota(jnp.int32, (tokens, tokens), 1)
    earlier = (ahead < behind).astype(jnp.bfloat16)
    prior = jnp.dot(hits.astype(jnp.bfloat16), earlier, preferred_element_type=jnp.float32)
    rows = []
    for k in range(TOP):
        slot = jnp.sum(jnp.where(named[k], prior, 0.0), axis=0, keepdims=True)
        rows.append(routes_ref[k : k + 1, :] * capacity + slot.astype(jnp.int32))
    return rows


def slot_masks(routes_ref, ep_size, capacity):
    tokens = routes_ref.shape[1]
    slots = lax.broadcasted_iota(jnp.int32, (ep_size * capacity, tokens), 0)
    return [slots == row for row in slot_rows(routes_ref, ep_size, capacity)]


def place_grads(sizes, routes_ref, weights_ref, g_ref, rows, rows_hbm, sems):
    masks = slot_masks(routes_ref, *sizes)
    pick = functools.reduce(jnp.logical_or, masks).astype(jnp.bfloat16)
    scale = sum(
        jnp.sum(jnp.where(masks[k], weights_ref[k : k + 1, :], 0.0), axis=1, keepdims=True)
        for k in range(TOP)
    )
    half = rows.shape[1] // 2
    copies = []
    for i in range(2):
        at = pl.ds(i * half, half)
        placed = jnp.dot(pick, g_ref[:, at], preferred_element_type=jnp.float32)
        rows[:, at] = (placed * scale).astype(jnp.bfloat16)
        copies.append(pltpu.make_async_copy(rows.at[:, at], rows_hbm.at[:, at], sems.at[1 + i]))
        copies[-1].start()
    for copy in copies:
        copy.wait()


def dispatch_tokens_kernel(
    sizes, routes_ref, weights_ref, x_ref, g_hbm, out_ref, early_hbm, pick_ref, g_ref, rows, sems
):
    step = pl.program_id(0)
    first = step == 0
    early = lax.axis_index("tp") == 0
    load = pltpu.make_async_copy(g_hbm, g_ref, sems.at[0])

    @pl.when(jnp.logical_and(early, first))
    def _():
        load.start()

    @pl.when(first)
    def _():
        masks = slot_masks(routes_ref, *sizes)
        pick_ref[...] = functools.reduce(jnp.logical_or, masks).astype(jnp.bfloat16)

    out_ref[...] = jnp.dot(
        pick_ref[...], x_ref[...], preferred_element_type=jnp.float32
    ).astype(jnp.bfloat16)

    @pl.when(jnp.logical_and(early, step == pl.num_programs(0) - 1))
    def _():
        load.wait()
        place_grads(sizes, routes_ref, weights_ref, g_ref, rows, early_hbm, sems)


def dispatch_grads_kernel(
    sizes, routes_ref, weights_ref, g_hbm, early_hbm, out_hbm, g_ref, rows, sems
):
    @pl.when(lax.axis_index("tp") != 0)
    def _():
        load = pltpu.make_async_copy(g_hbm, g_ref, sems.at[0])
        load.start()
        load.wait()
        place_grads(sizes, routes_ref, weights_ref, g_ref, rows, out_hbm, sems)


def split_weight(value):
    high = value.astype(jnp.bfloat16)
    low = (value - high.astype(jnp.float32)).astype(jnp.bfloat16)
    return high, low


def collect_dot(picked, rows):
    return lax.dot_general(
        picked, rows, (((0,), (0,)), ((), ())), preferred_element_type=jnp.float32
    )


def combine_outputs_kernel(
    ep_size, capacity, routes_ref, weights_ref, upstream_ref, rows_ref, mixed_ref, route_ref, pick_ref, acc
):
    step = pl.program_id(0)
    masks = slot_masks(routes_ref, ep_size, capacity)
    weighted = sum(
        jnp.where(masks[k], weights_ref[k : k + 1, :], 0.0) for k in range(TOP)
    )
    high, low = split_weight(weighted)
    rows = rows_ref[...]
    mixed_ref[...] = (collect_dot(high, rows) + collect_dot(low, rows)).astype(jnp.bfloat16)

    @pl.when(step == 0)
    def _():
        acc[...] = jnp.zeros_like(acc)
        pick = functools.reduce(jnp.logical_or, masks).astype(jnp.float32)
        pick_ref[...] = pick.T.astype(jnp.bfloat16)

    acc[...] += lax.dot_general(
        rows, upstream_ref[...], (((1,), (1,)), ((), ())), preferred_element_type=jnp.float32
    )

    @pl.when(step == pl.num_programs(0) - 1)
    def _():
        for k in range(TOP):
            route_ref[k : k + 1, :] = jnp.sum(
                jnp.where(masks[k], acc[...], 0.0), axis=0, keepdims=True
            )


def combine_grads_kernel(pick_ref, rows_ref, out_ref):
    out_ref[...] = jnp.dot(
        pick_ref[...], rows_ref[...], preferred_element_type=jnp.float32
    ).astype(jnp.bfloat16)


def rows_dot(a, b):
    return jnp.dot(a, b, preferred_element_type=jnp.float32)


def turned_dot(a, b):
    return lax.dot_general(a, b, (((1,), (1,)), ((), ())), preferred_element_type=jnp.float32)


def weight_dot(a, b):
    return lax.dot_general(a, b, (((0,), (0,)), ((), ())), preferred_element_type=jnp.float32)


def add_up(first, acc, value):
    @pl.when(first)
    def _():
        acc[...] = value

    @pl.when(jnp.logical_not(first))
    def _():
        acc[...] += value


def beside(*refs):
    return jnp.concatenate([ref[...] for ref in refs], axis=1)


def stacked(*refs):
    return jnp.concatenate([ref[...] for ref in refs], axis=0)


def forward_kernel(
    steps,
    x_ref,
    gate_a,
    gate_b,
    up_a,
    up_b,
    down_a,
    down_b,
    rows_out,
    pre,
    hidden_a,
    hidden_b,
    hidden,
):
    step = pl.program_id(0)
    units = gate_a.shape[1]
    both = 2 * units

    @pl.when(step < steps)
    def _():
        add_up(step == 0, pre, rows_dot(x_ref[...], beside(gate_a, gate_b, up_a, up_b)))

    @pl.when(step == steps - 1)
    def _():
        gate_pre = pre[:, :both]
        made = (gate_pre * jax.nn.sigmoid(gate_pre) * pre[:, both:]).astype(jnp.bfloat16)
        hidden[...] = made
        hidden_a[...] = made[:, :units]
        hidden_b[...] = made[:, units:]

    @pl.when(step >= steps)
    def _():
        rows_out[...] = rows_dot(hidden[...], stacked(down_a, down_b)).astype(jnp.bfloat16)


def backward_kernel(
    steps,
    g_ref,
    pre,
    down_a,
    down_b,
    gate_a,
    gate_b,
    up_a,
    up_b,
    rows_out,
    d_gate_a,
    d_gate_b,
    d_up_a,
    d_up_b,
    d_hidden,
    d_both,
):
    step = pl.program_id(0)
    units = gate_a.shape[1]
    both = 2 * units

    @pl.when(step < steps)
    def _():
        add_up(step == 0, d_hidden, turned_dot(g_ref[...], stacked(down_a, down_b)))

    @pl.when(step == steps - 1)
    def _():
        gate_pre = pre[:, :both]
        sigmoid_gate = jax.nn.sigmoid(gate_pre)
        d_rows = d_hidden[...]
        d_gate = (
            d_rows * pre[:, both:] * sigmoid_gate * (1.0 + gate_pre * (1.0 - sigmoid_gate))
        ).astype(jnp.bfloat16)
        d_up = (d_rows * gate_pre * sigmoid_gate).astype(jnp.bfloat16)
        d_both[:, :both] = d_gate
        d_both[:, both:] = d_up
        d_gate_a[...] = d_gate[:, :units]
        d_gate_b[...] = d_gate[:, units:]
        d_up_a[...] = d_up[:, :units]
        d_up_b[...] = d_up[:, units:]

    @pl.when(step >= steps)
    def _():
        rows_out[...] = turned_dot(d_both[...], beside(gate_a, gate_b, up_a, up_b)).astype(
            jnp.bfloat16
        )


def expert_calls(slots, width, units, block, params):
    steps = width // block
    bf16, f32 = jnp.bfloat16, jnp.float32
    first = lambda i: jnp.minimum(i, steps - 1)
    second = lambda i: jnp.maximum(i - steps, 0)
    rows = lambda at: pl.BlockSpec((slots, block), lambda i: (0, at(i)))
    wide = lambda at: pl.BlockSpec((units, block), lambda i: (0, at(i)))
    tall = lambda at: pl.BlockSpec((block, units), lambda i: (at(i), 0))
    held = whole((slots, units))
    pre = whole((slots, 4 * units))
    array = lambda columns, dtype: jax.ShapeDtypeStruct((slots, columns), dtype)
    call = functools.partial(
        pl.pallas_call, grid=(2 * steps,), compiler_params=params, cost_estimate=FEW
    )
    forward = call(
        functools.partial(forward_kernel, steps),
        in_specs=[rows(first)] + [tall(first)] * 4 + [wide(second)] * 2,
        out_specs=[rows(second), pre, held, held],
        out_shape=[array(width, bf16), array(4 * units, f32)] + [array(units, bf16)] * 2,
        scratch_shapes=[pltpu.VMEM((slots, 2 * units), bf16)],
        name="forward",
    )
    backward = call(
        functools.partial(backward_kernel, steps),
        in_specs=[rows(first), pre] + [wide(first)] * 2 + [tall(second)] * 4,
        out_specs=[rows(second)] + [held] * 4,
        out_shape=[array(width, bf16)] + [array(units, bf16)] * 4,
        scratch_shapes=[
            pltpu.VMEM((slots, 2 * units), f32), pltpu.VMEM((slots, 4 * units), bf16)
        ],
        name="backward",
    )
    return forward, backward


def gate_up_kernel(x_near, x_far, d_gate_near, d_gate_far, d_up_near, d_up_far, gate_out, up_out):
    units = d_gate_near.shape[1]
    total = weight_dot(x_near[...], beside(d_gate_near, d_up_near)) + weight_dot(
        x_far[...], beside(d_gate_far, d_up_far)
    )
    gate_out[...] = total[:, :units].astype(jnp.bfloat16)
    up_out[...] = total[:, units:].astype(jnp.bfloat16)


def down_kernel(g_near, g_far, hidden_near, hidden_far, down_out):
    down_out[...] = (
        weight_dot(hidden_near[...], g_near[...]) + weight_dot(hidden_far[...], g_far[...])
    ).astype(jnp.bfloat16)


def cost(products, *arrays):
    moved = sum(a.size * a.dtype.itemsize for a in arrays)
    return pl.CostEstimate(flops=2 * products, bytes_accessed=moved, transcendentals=0)


def grads_of_gate_up(near, far, d_gate, d_up, block, params):
    slots, width = near.shape
    units = d_gate[0].shape[1]
    held = whole((slots, units))
    tall = pl.BlockSpec((block, units), lambda i: (i, 0))
    rows = pl.BlockSpec((slots, block), lambda i: (0, i))
    return pl.pallas_call(
        gate_up_kernel,
        grid=(width // block,),
        in_specs=[rows, rows] + [held] * 4,
        out_specs=[tall, tall],
        out_shape=[jax.ShapeDtypeStruct((width, units), jnp.bfloat16)] * 2,
        compiler_params=params,
        cost_estimate=cost(4 * slots * width * units, near, far),
        name="grad_gate_up",
    )(near, far, *d_gate, *d_up)


def grads_of_down(near, far, hidden, block, params):
    slots, width = near.shape
    units = hidden[0].shape[1]
    held = whole((slots, units))
    rows = pl.BlockSpec((slots, block), lambda i: (0, i))
    return pl.pallas_call(
        down_kernel,
        grid=(width // block,),
        in_specs=[rows, rows, held, held],
        out_specs=pl.BlockSpec((units, block), lambda i: (0, i)),
        out_shape=jax.ShapeDtypeStruct((units, width), jnp.bfloat16),
        compiler_params=params,
        cost_estimate=cost(2 * slots * width * units, near, far),
        name="grad_down",
    )(near, far, *hidden)


def whole(shape):
    return pl.BlockSpec(shape, lambda i: (0, 0))


def columns(rows, width):
    return pl.BlockSpec((rows, width), lambda i: (0, i))


def to_experts(rows, ep_size):
    blocks = rows.reshape(ep_size, -1, rows.shape[1])
    return lax.all_to_all(blocks, "ep", split_axis=0, concat_axis=0, tiled=True).reshape(rows.shape)


def swap(rows):
    return lax.ppermute(rows, "tp", SWAP)


def on_device(tokens, upstream, routes, route_weights, gate_weight, up_weight, down_weight):
    ep_size = lax.axis_size("ep")
    token_count, width = tokens.shape
    capacity = 2 * token_count * TOP // ep_size
    slots = ep_size * capacity
    block = min(1024, width // 2)
    broad = min(2048, width // 2)
    grid = (width // broad,)
    routes_t = routes.T
    weights_t = route_weights.T
    small = whole((TOP, token_count))
    params = pltpu.CompilerParams(vmem_limit_bytes=56 * 1024 * 1024)
    sizes = (ep_size, capacity)

    anywhere = pl.BlockSpec(memory_space=pl.ANY)
    inside = pl.BlockSpec(memory_space=pltpu.VMEM)
    sent = jax.ShapeDtypeStruct((slots, width), jnp.bfloat16)
    place = [
        pltpu.VMEM((token_count, width), jnp.bfloat16),
        pltpu.VMEM((slots, width), jnp.bfloat16),
        pltpu.SemaphoreType.DMA((3,)),
    ]
    sent_tokens, early_grads = pl.pallas_call(
        functools.partial(dispatch_tokens_kernel, sizes),
        grid=grid,
        in_specs=[small, small, columns(token_count, broad), anywhere],
        out_specs=[columns(slots, broad), anywhere],
        out_shape=[sent, sent],
        scratch_shapes=[pltpu.VMEM((slots, token_count), jnp.bfloat16)] + place,
        compiler_params=params,
        name="dispatch_tokens",
    )(routes_t, weights_t, tokens, upstream)
    gate_mat, up_mat, down_mat = gate_weight[0], up_weight[0], down_weight[0]
    gate = (gate_mat, swap(gate_mat))
    up = (up_mat, swap(up_mat))
    down = (down_mat, swap(down_mat))
    gate_b, up_b, down_b, weights_late = lax.optimization_barrier(
        (gate[1], up[1], down[1], weights_t)
    )
    gate, up, down = (gate_mat, gate_b), (up_mat, up_b), (down_mat, down_b)
    sent_grads = pl.pallas_call(
        functools.partial(dispatch_grads_kernel, sizes),
        in_specs=[inside, inside, anywhere, anywhere],
        out_specs=anywhere,
        out_shape=sent,
        input_output_aliases={3: 0},
        scratch_shapes=place,
        compiler_params=params,
        name="dispatch_grads",
    )(routes_t, weights_late, upstream, early_grads)
    forward, backward = expert_calls(slots, width, gate_mat.shape[1], block, params)

    inputs = to_experts(sent_tokens, ep_size)
    inputs, sent_grads = lax.optimization_barrier((inputs, sent_grads))
    grads = to_experts(sent_grads, ep_size)
    out, pre, hidden_a, hidden_b = forward(inputs, *gate, *up, *down)
    grads, out = lax.optimization_barrier((grads, out))
    out_home = to_experts(out, ep_size)
    back, d_gate_a, d_gate_b, d_up_a, d_up_b = backward(grads, pre, *down, *gate, *up)
    out_home, back, d_up_a, d_gate_a, hidden_a = lax.optimization_barrier(
        (out_home, back, d_up_a, d_gate_a, hidden_a)
    )
    back_home = to_experts(back, ep_size)

    grad_gate, grad_up = grads_of_gate_up(
        inputs, swap(inputs), (d_gate_a, swap(d_gate_b)), (d_up_a, swap(d_up_b)), block, params
    )
    grad_down = grads_of_down(grads, swap(grads), (hidden_a, swap(hidden_b)), block, params)
    mixed, grad_route, picked = pl.pallas_call(
        functools.partial(combine_outputs_kernel, *sizes),
        grid=grid,
        in_specs=[small, small, columns(token_count, broad), columns(slots, broad)],
        out_specs=[columns(token_count, broad), small, whole((token_count, slots))],
        out_shape=[
            jax.ShapeDtypeStruct((token_count, width), jnp.bfloat16),
            jax.ShapeDtypeStruct((TOP, token_count), jnp.float32),
            jax.ShapeDtypeStruct((token_count, slots), jnp.bfloat16),
        ],
        scratch_shapes=[pltpu.VMEM((slots, token_count), jnp.float32)],
        compiler_params=params,
        cost_estimate=cost(3 * token_count * slots * width, upstream, out_home),
        name="combine_outputs",
    )(routes_t, weights_t, upstream, out_home)
    grad_tokens = pl.pallas_call(
        combine_grads_kernel,
        grid=grid,
        in_specs=[whole((token_count, slots)), columns(slots, broad)],
        out_specs=columns(token_count, broad),
        out_shape=jax.ShapeDtypeStruct((token_count, width), jnp.bfloat16),
        compiler_params=params,
        name="combine_grads",
    )(picked, back_home)
    return (mixed, grad_tokens, grad_route.T, grad_gate[None], grad_up[None], grad_down[None])


def solution(mesh):
    rows = P(("tp", "ep"), None)
    split_columns = P("ep", None, "tp")
    split_rows = P("ep", "tp", None)
    return jax.shard_map(
        on_device,
        mesh=mesh,
        in_specs=(rows, rows, rows, rows, split_columns, split_columns, split_rows),
        out_specs=(rows, rows, rows, split_columns, split_columns, split_rows),
        check_vma=False,
    )
```
